32 devices in a mesh: cand: 2 (over y), hid: 16 (over z, x, core).
Axes of the slice: x: 2, y: 2, z: 4, core: 2. Of those that a mesh axis runs over, the one named last changes fastest.
Arguments:
- tokens: bfloat16 [32, 8192], P(('cand', 'hid')), parts along dimension 0, may hold values from -6 to 6
- teacher: bfloat16 [32, 8192], P(('cand', 'hid')), parts along dimension 0, may hold values from -4 to 4
- w_gate: bfloat16 [8192, 16384], P(None, 'hid'), may hold values from -0.0625 to 0.0625
- w_up: bfloat16 [8192, 16384], P(None, 'hid'), may hold values from -0.0625 to 0.0625
- w_down: bfloat16 [16384, 8192], P('hid'), may hold values from -0.046875 to 0.046875
- tile_scale: float32 [3, 128, 64], P(None, 'hid'), may hold values from 0.0005 to 0.005
- block_mask: int32 [6, 128, 64], P('cand', 'hid'), parts along dimension 0, may hold values from 0 to 1, as said below
- bit_width: int32 [6], P('cand'), parts along dimension 0, may hold values from 3 to 6
Outputs:
- student: bfloat16 [32, 8192], P(('cand', 'hid')), parts along dimension 0
- token_grad: bfloat16 [32, 8192], P(('cand', 'hid')), parts along dimension 0
- grad_gate: bfloat16 [16384, 16384], P('cand', 'hid'), parts along dimension 0
- grad_up: bfloat16 [16384, 16384], P('cand', 'hid'), parts along dimension 0
- grad_down: bfloat16 [32768, 8192], P(('cand', 'hid')), parts along dimension 0
The draws below stay inside these ranges and needn't reach their ends.
There are 2 independent parts, one for each index of `cand`. The reference program is written for one: setup_inputs(seed, part) draws one part's arguments, and reference() takes and returns one part's arrays. A program takes and returns all parts, laid end to end along the dimension named above; an argument that names none is the same for every part. Nothing has to cross between parts.
Inputs may be any that keep to these rules, and one draw needn't show every extreme that they name: `block_mask`: each row of 64 width tiles of one matrix and hidden tile keeps 16 to 48 tiles; in every draw some row of each matrix keeps exactly 48.
All inputs are finite; a program needn't handle non-finite values.
Results may differ from the reference program's by a relative error of at most 0.0067.
Values may be sent and summed in bfloat16 or wider, within the bound.
A program may use at most 384 MiB of HBM per device.

```python
import math
import jax
import jax.numpy as jnp

D = 8192
FF = 16384
BLOCK = 128
TOKENS = 16
WB = 64
HB = 128
LEAST_KEPT = 16
MOST_KEPT = 48


def draw_block_mask(key, part):
    key = jax.random.fold_in(key, 11)
    count_key, pick_key, order_key = jax.random.split(key, 3)
    counts = jax.random.randint(count_key, (3, HB), LEAST_KEPT, MOST_KEPT + 1)
    chosen = jax.random.randint(pick_key, (3,), 0, HB)
    positions = jnp.arange(HB)[None, :]
    counts = jnp.where(positions == chosen[:, None], MOST_KEPT, counts)
    row_keys = jax.random.split(order_key, 3 * HB)
    orders = jax.vmap(lambda one_key: jax.random.permutation(one_key, WB))(row_keys)
    orders = orders.reshape(3, HB, WB)
    return (orders < counts[:, :, None]).astype(jnp.int32)


def level_of(rng, shape, cuts, low, top_value):
    factor_of, own = 1.0, jax.random.fold_in(rng, 6)
    for dim, blocks in cuts:
        draws = jnp.exp(jax.random.uniform(jax.random.fold_in(own, dim), (blocks,), jnp.float32, low / len(cuts), top_value / len(cuts)))
        factor_of = factor_of * jnp.repeat(draws, shape[dim] // blocks).reshape([-1 if axis == dim else 1 for axis in range(len(shape))])
    return factor_of


def normal_values(stream_key, dims, width, most, cuts=(), kind=jnp.bfloat16):
    result = width * jax.random.normal(stream_key, dims, jnp.float32)
    if cuts:
        result = result * level_of(stream_key, dims, cuts, -0.22, 0.18)
    return jnp.clip(result, -most, most).astype(kind)


def setup_inputs(seed: int = 0, part: int = 0) -> dict:
    key_of = jax.random.split(jax.random.key(seed), 9)
    part_splits = jax.random.split(jax.random.fold_in(key_of[8], part), 9)
    return {
        "tokens": normal_values(part_splits[0], (TOKENS, D), 1.0, 6.0, ((0, 16),)),
        "teacher": normal_values(part_splits[1], (TOKENS, D), 0.25, 4.0, ((0, 16),)),
        "w_gate": normal_values(key_of[2], (D, FF), D ** -0.5, 0.0625, ((1, 16),)),
        "w_up": normal_values(key_of[3], (D, FF), D ** -0.5, 0.0625, ((1, 16),)),
        "w_down": normal_values(key_of[4], (FF, D), FF ** -0.5, 0.046875, ((0, 16),)),
        "tile_scale": jnp.clip(jnp.exp(math.log(0.005) - 2.30258502 * jax.random.uniform(key_of[5], (3, HB, WB), jnp.float32) ** level_of(key_of[5], (3, HB, WB), ((1, 16),), -0.2, 0.2)), 0.0005, 0.005),
        "block_mask": draw_block_mask(jax.random.fold_in(jax.random.fold_in(key_of[8], part), 71), part),
        "bit_width": jax.random.randint(part_splits[7], (3,), 3, 7).astype(jnp.int32),
    }


def expand_in(tiles):
    return jnp.repeat(jnp.repeat(tiles.T, BLOCK, axis=0), BLOCK, axis=1)


def expand_out(tiles):
    return jnp.repeat(jnp.repeat(tiles, BLOCK, axis=0), BLOCK, axis=1)


def effective(weight, clip_bound, kept_mask):
    clipped = jnp.clip(weight.astype(jnp.float32), -clip_bound, clip_bound)
    return (kept_mask * clipped).astype(jnp.bfloat16)


def reference(tokens, teacher, w_gate, w_up, w_down, tile_scale, block_mask, bit_width):
    top_level = (jnp.left_shift(1, bit_width - 1) - 1).astype(jnp.float32)
    mask_float = block_mask.astype(jnp.float32)
    gate_mask = expand_in(mask_float[0])
    up_mask = expand_in(mask_float[1])
    down_mask = expand_out(mask_float[2])
    gate_eff = effective(w_gate, expand_in(tile_scale[0] * top_level[0]), gate_mask)
    up_eff = effective(w_up, expand_in(tile_scale[1] * top_level[1]), up_mask)
    down_eff = effective(w_down, expand_out(tile_scale[2] * top_level[2]), down_mask)
    gate_pre = jnp.dot(tokens, gate_eff, preferred_element_type=jnp.float32)
    up_pre = jnp.dot(tokens, up_eff, preferred_element_type=jnp.float32)
    sig_gate = jax.nn.sigmoid(gate_pre)
    activated = gate_pre * sig_gate
    hidden = (activated * up_pre).astype(jnp.bfloat16)
    student_sum = jnp.dot(hidden, down_eff, preferred_element_type=jnp.float32)
    student = student_sum.astype(jnp.bfloat16)
    residual = (student_sum - teacher.astype(jnp.float32)).astype(jnp.bfloat16)
    d_hidden = jnp.dot(residual, down_eff.T, preferred_element_type=jnp.float32)
    d_gate = (d_hidden * up_pre * sig_gate * (1.0 + gate_pre * (1.0 - sig_gate))).astype(jnp.bfloat16)
    d_up = (d_hidden * activated).astype(jnp.bfloat16)
    grad_gate = (jnp.dot(tokens.T, d_gate, preferred_element_type=jnp.float32) * gate_mask).astype(jnp.bfloat16)
    grad_up = (jnp.dot(tokens.T, d_up, preferred_element_type=jnp.float32) * up_mask).astype(jnp.bfloat16)
    grad_down = (jnp.dot(hidden.T, residual, preferred_element_type=jnp.float32) * down_mask).astype(jnp.bfloat16)
    token_sum = jnp.dot(d_gate, gate_eff.T, preferred_element_type=jnp.float32) + jnp.dot(d_up, up_eff.T, preferred_element_type=jnp.float32)
    token_grad = token_sum.astype(jnp.bfloat16)
    return (student, token_grad, grad_gate, grad_up, grad_down)
```

```python
import functools

import jax
import jax.numpy as jnp
from jax import lax
from jax.experimental import pallas as pl
from jax.experimental.pallas import tpu as pltpu
from jax.sharding import PartitionSpec as P

BLOCK = 128
VMEM_BYTES = 56 * 1024 * 1024
F32 = jnp.float32
BF16 = jnp.bfloat16


def peer(index):
    return (lax.axis_index("cand"), index)


def greet(chips):
    me = lax.axis_index("hid")
    chip, core = me // 2, me % 2
    barrier = pltpu.get_barrier_semaphore()
    for k in range(1, chips):
        pl.semaphore_signal(
            barrier,
            inc=1,
            device_id=peer(2 * lax.rem(chip + k, chips) + core),
            device_id_type=pl.DeviceIdType.MESH,
        )
    pl.semaphore_signal(
        barrier, inc=1, device_id=peer(2 * chip + 1 - core), device_id_type=pl.DeviceIdType.MESH
    )
    pl.semaphore_wait(barrier, chips)


def remote(src, dst, send_sem, recv_sem, index):
    return pltpu.make_async_remote_copy(
        src_ref=src,
        dst_ref=dst,
        send_sem=send_sem,
        recv_sem=recv_sem,
        device_id=peer(index),
        device_id_type=pl.DeviceIdType.MESH,
    )


def gather_blocks(chips, held, far_send, far_recv, near_send, near_recv):
    me = lax.axis_index("hid")
    chip, core = me // 2, me % 2
    beside = 2 * chip + 1 - core
    started = []
    for k in range(1, chips):
        to = 2 * lax.rem(chip + k, chips) + core
        copy = remote(held.at[me], held.at[me], far_send.at[k], far_recv.at[k], to)
        copy.start()
        started.append(copy)
    own = remote(held.at[me], held.at[me], near_send.at[0], near_recv.at[0], beside)
    own.start()
    passed = [own]
    for k in range(1, chips):
        source = 2 * lax.rem(chip - k + chips, chips) + core
        arrived = remote(
            held.at[source], held.at[source], far_send.at[k], far_recv.at[k], source
        )
        arrived.wait_recv()
        onward = remote(
            held.at[source], held.at[source], near_send.at[k], near_recv.at[k], beside
        )
        onward.start()
        passed.append(onward)
    for k in range(chips):
        block = 2 * lax.rem(chip - k + chips, chips) + 1 - core
        remote(
            held.at[block], held.at[block], near_send.at[k], near_recv.at[k], beside
        ).wait_recv()
    for copy in started + passed:
        copy.wait_send()


def scatter_sum(chips, part, near_in, out_slot, far_in, far_send, far_recv, near_send, near_recv):
    me = lax.axis_index("hid")
    chip, core = me // 2, me % 2
    beside = 2 * chip + 1 - core
    near = []
    for k in range(1, chips + 1):
        to = lax.rem(chip + k, chips)
        copy = remote(
            part.at[1 - core, to], near_in.at[to], near_send.at[k - 1], near_recv.at[k - 1], beside
        )
        copy.start()
        near.append(copy)
    far = []
    for k in range(1, chips):
        to = lax.rem(chip + k, chips)
        near[k - 1].wait_recv()
        out_slot[k] = (part[core, to].astype(F32) + near_in[to].astype(F32)).astype(BF16)
        copy = remote(
            out_slot.at[k], far_in.at[k], far_send.at[k], far_recv.at[k], 2 * to + core
        )
        copy.start()
        far.append(copy)
    near[chips - 1].wait_recv()
    total = part[core, chip].astype(F32) + near_in[chip].astype(F32)
    for k in range(1, chips):
        far[k - 1].wait_recv()
        total = total + far_in[k].astype(F32)
    for copy in near + far:
        copy.wait_send()
    return total


def gather_kernel(chips, own, out, held, fs, fr, ns, nr):
    held[lax.axis_index("hid")] = own[...]
    greet(chips)
    gather_blocks(chips, held, fs, fr, ns, nr)
    out[...] = held[...]


def residual_kernel(
    chips, part, teacher, student, out, held, near_in, out_slot, far_in, fs, fr, ns, nr, fs2, fr2, ns2, nr2
):
    greet(chips)
    total = scatter_sum(chips, part, near_in, out_slot, far_in, fs, fr, ns, nr)
    student[...] = total.astype(BF16)
    held[lax.axis_index("hid")] = (total - teacher[...].astype(F32)).astype(BF16)
    gather_blocks(chips, held, fs2, fr2, ns2, nr2)
    out[...] = held[...]


def scatter_kernel(chips, part, out, near_in, out_slot, far_in, fs, fr, ns, nr):
    greet(chips)
    out[...] = scatter_sum(chips, part, near_in, out_slot, far_in, fs, fr, ns, nr).astype(BF16)


def link_sems(chips):
    return [pltpu.SemaphoreType.DMA((chips,))] * 4


def in_vmem(count):
    return [pl.BlockSpec(memory_space=pltpu.VMEM)] * count


def exchange(body, operands, out_shape, scratch, cid):
    return pl.pallas_call(
        body,
        out_shape=out_shape,
        in_specs=in_vmem(len(operands)),
        out_specs=jax.tree.map(lambda _: pl.BlockSpec(memory_space=pltpu.VMEM), out_shape),
        scratch_shapes=scratch,
        compiler_params=pltpu.CompilerParams(collective_id=cid, has_side_effects=True),
    )(*operands)


def contract_first(left, right):
    return lax.dot_general(
        left, right, (((0,), (0,)), ((), ())), preferred_element_type=F32
    )


def contract_last(left, right):
    return lax.dot_general(
        left, right, (((1,), (1,)), ((), ())), preferred_element_type=F32
    )


def one_hot(tiles, width):
    row = lax.broadcasted_iota(jnp.int32, (tiles, width), 0)
    column = lax.broadcasted_iota(jnp.int32, (tiles, width), 1)
    return (column // BLOCK == row).astype(F32).astype(BF16)


def spread_rows(tiles, into):
    count, per, wide = into.shape
    full = contract_first(tiles, one_hot(tiles.shape[0], wide))
    for g in range(count):
        into[g] = full[g * per : (g + 1) * per]


def spread_columns(tiles, into):
    count, per, wide = into.shape
    for g in range(count):
        cut = wide // BLOCK
        into[g] = jnp.dot(
            tiles[:, g * cut : (g + 1) * cut],
            one_hot(cut, wide),
            preferred_element_type=F32,
        )


def clipped(weight, bounds):
    pieces = []
    for j in range(weight.shape[0] // BLOCK):
        bound = bounds[j : j + 1].astype(BF16)
        piece = weight[j * BLOCK : (j + 1) * BLOCK]
        pieces.append(jnp.maximum(jnp.minimum(piece, bound), -bound))
    return jnp.concatenate(pieces, axis=0) if len(pieces) > 1 else pieces[0]


def to_rows(blocks, flat, into):
    tokens, tiles = blocks.shape[0], blocks.shape[1]
    flat[...] = blocks[...].astype(F32).reshape(flat.shape)
    count, _, wide = into.shape
    cut = wide // BLOCK
    for w in range(tiles):
        piece = flat[pl.ds(w, tokens, stride=tiles), :].astype(BF16)
        into[w // cut, :, (w % cut) * BLOCK : (w % cut + 1) * BLOCK] = piece


def put_columns(flat, value, first, tiles):
    tokens = value.shape[0]
    for j in range(value.shape[1] // BLOCK):
        flat[pl.ds(first + j, tokens, stride=tiles), :] = value[:, j * BLOCK : (j + 1) * BLOCK]


def to_shares(flat, out):
    _, chips, per, _ = out.shape
    for d in range(2 * chips):
        out[d % 2, d // 2] = flat[d * per : (d + 1) * per].astype(BF16)


def forward_kernel(
    steps, tiles, tok, wg, wu, wd, bound, part, gate_pre, up_pre, hidden, flat, rows, bg, bu, bd
):
    i = pl.program_id(0)

    @pl.when(i == 0)
    def _():
        to_rows(tok, flat, rows)
        spread_rows(bound[0], bg)
        spread_rows(bound[1], bu)
        spread_columns(bound[2], bd)
        gate_pre[...] = jnp.zeros_like(gate_pre)
        up_pre[...] = jnp.zeros_like(up_pre)

    @pl.when(i < steps)
    def _():
        gate_pre[...] += jnp.dot(rows[i], clipped(wg[...], bg[i]), preferred_element_type=F32)
        up_pre[...] += jnp.dot(rows[i], clipped(wu[...], bu[i]), preferred_element_type=F32)

    @pl.when(i == steps - 1)
    def _():
        gate = gate_pre[...]
        hidden[...] = (gate * jax.nn.sigmoid(gate) * up_pre[...]).astype(BF16)

    @pl.when(i >= steps)
    def _():
        c = i - steps
        value = jnp.dot(hidden[...], clipped(wd[...], bd[c]), preferred_element_type=F32)
        put_columns(flat, value, c * (value.shape[1] // BLOCK), tiles)

    @pl.when(i == 2 * steps - 1)
    def _():
        to_shares(flat, part)


def backward_kernel(
    steps, tiles, res, wg, wu, wd, bound, gate_pre, up_pre, part, d_gate, d_up, flat, rows, bg, bu, bd, d_hidden
):
    i = pl.program_id(0)

    @pl.when(i == 0)
    def _():
        to_rows(res, flat, rows)
        spread_rows(bound[0], bg)
        spread_rows(bound[1], bu)
        spread_columns(bound[2], bd)
        d_hidden[...] = jnp.zeros_like(d_hidden)

    @pl.when(i < steps)
    def _():
        d_hidden[...] += contract_last(rows[i], clipped(wd[...], bd[i]))

    @pl.when(i == steps - 1)
    def _():
        gate = gate_pre[...]
        sig = jax.nn.sigmoid(gate)
        d_gate[...] = (d_hidden[...] * up_pre[...] * sig * (1.0 + gate * (1.0 - sig))).astype(BF16)
        d_up[...] = (d_hidden[...] * (gate * sig)).astype(BF16)

    @pl.when(i >= steps)
    def _():
        c = i - steps
        value = contract_last(d_gate[...], clipped(wg[...], bg[c])) + contract_last(
            d_up[...], clipped(wu[...], bu[c])
        )
        put_columns(flat, value, c * (value.shape[1] // BLOCK), tiles)

    @pl.when(i == 2 * steps - 1)
    def _():
        to_shares(flat, part)


def outer(left, right, mask, out):
    for j in range(left.shape[1] // BLOCK):
        kept = right * mask[j : j + 1].astype(BF16)
        out[j * BLOCK : (j + 1) * BLOCK] = contract_first(
            left[:, j * BLOCK : (j + 1) * BLOCK], kept
        ).astype(BF16)


def grad_kernel(tok, res, hidden, d_gate, d_up, mask, gg, gu, gd, flat, rows, rows2, mg, mu, md):
    i = pl.program_id(0)

    @pl.when(i == 0)
    def _():
        to_rows(tok, flat, rows)
        to_rows(res, flat, rows2)
        spread_rows(mask[0], mg)
        spread_rows(mask[1], mu)
        spread_columns(mask[2], md)

    outer(rows[i], d_gate[...], mg[i], gg)
    outer(rows[i], d_up[...], mu[i], gu)
    outer(hidden[...], rows2[i], md[i], gd)


def per_device(n, tokens, teacher, w_gate, w_up, w_down, tile_scale, block_mask, bit_width):
    chips = n // 2
    mine, width = tokens.shape
    tiles = width // BLOCK
    all_tokens = n * mine
    hid = w_gate.shape[1]
    hid_tiles = hid // BLOCK
    cut = 512
    steps = width // cut
    per = cut // BLOCK
    share = mine * tiles

    level = (jnp.left_shift(1, bit_width - 1) - 1).astype(F32)
    mask = block_mask.astype(F32)
    bound = (tile_scale * level[:, None, None] * mask).astype(BF16)
    mask = mask.astype(BF16)

    block = jax.ShapeDtypeStruct((share, BLOCK), BF16)
    blocks = jax.ShapeDtypeStruct((n, share, BLOCK), BF16)
    held = pltpu.VMEM((n, share, BLOCK), BF16)
    some = pltpu.VMEM((chips, share, BLOCK), BF16)

    tok = exchange(
        functools.partial(gather_kernel, chips),
        (tokens.reshape(share, BLOCK),),
        blocks,
        [held] + link_sems(chips),
        0,
    ).reshape(all_tokens, tiles, BLOCK)

    whole = lambda shape: pl.BlockSpec(shape, lambda i: (0,) * len(shape))
    first = lambda i: jnp.minimum(i, steps - 1)
    second = lambda i: jnp.maximum(i - steps, 0)
    tok_spec = whole((all_tokens, tiles, BLOCK))
    pre_spec = whole((all_tokens, hid))
    part_shape = (2, chips, share, BLOCK)
    bound_spec = whole((3, hid_tiles, tiles))
    flat = pltpu.VMEM((all_tokens * tiles, BLOCK), F32)
    rows = pltpu.VMEM((steps, all_tokens, cut), BF16)
    row_tiles = pltpu.VMEM((steps, per, hid), F32)
    column_tiles = pltpu.VMEM((steps, hid_tiles, cut), F32)
    params = pltpu.CompilerParams(
        dimension_semantics=("arbitrary",), vmem_limit_bytes=VMEM_BYTES
    )
    pre = jax.ShapeDtypeStruct((all_tokens, hid), F32)
    low = jax.ShapeDtypeStruct((all_tokens, hid), BF16)

    part, gate_pre, up_pre, hidden = pl.pallas_call(
        functools.partial(forward_kernel, steps, tiles),
        grid=(2 * steps,),
        in_specs=[
            tok_spec,
            pl.BlockSpec((cut, hid), lambda i: (first(i), 0)),
            pl.BlockSpec((cut, hid), lambda i: (first(i), 0)),
            pl.BlockSpec((hid, cut), lambda i: (0, second(i))),
            bound_spec,
        ],
        out_specs=[whole(part_shape), pre_spec, pre_spec, pre_spec],
        out_shape=[jax.ShapeDtypeStruct(part_shape, BF16), pre, pre, low],
        scratch_shapes=[flat, rows, row_tiles, row_tiles, column_tiles],
        compiler_params=params,
    )(tok, w_gate, w_up, w_down, bound)

    student, res = exchange(
        functools.partial(residual_kernel, chips),
        (part, teacher.reshape(share, BLOCK)),
        (block, blocks),
        [held, some, some, some] + link_sems(chips) + link_sems(chips),
        1,
    )
    res = res.reshape(all_tokens, tiles, BLOCK)

    part, d_gate, d_up = pl.pallas_call(
        functools.partial(backward_kernel, steps, tiles),
        grid=(2 * steps,),
        in_specs=[
            tok_spec,
            pl.BlockSpec((cut, hid), lambda i: (second(i), 0)),
            pl.BlockSpec((cut, hid), lambda i: (second(i), 0)),
            pl.BlockSpec((hid, cut), lambda i: (0, first(i))),
            bound_spec,
            pre_spec,
            pre_spec,
        ],
        out_specs=[whole(part_shape), pre_spec, pre_spec],
        out_shape=[jax.ShapeDtypeStruct(part_shape, BF16), low, low],
        scratch_shapes=[
            flat, rows, row_tiles, row_tiles, column_tiles, pltpu.VMEM((all_tokens, hid), F32)
        ],
        compiler_params=params,
    )(res, w_gate, w_up, w_down, bound, gate_pre, up_pre)

    token_grad = exchange(
        functools.partial(scatter_kernel, chips),
        (part,),
        block,
        [some, some, some] + link_sems(chips),
        2,
    )

    grad_gate, grad_up, grad_down = pl.pallas_call(
        grad_kernel,
        grid=(steps,),
        in_specs=[tok_spec, tok_spec, pre_spec, pre_spec, pre_spec, bound_spec],
        out_specs=[
            pl.BlockSpec((cut, hid), lambda i: (i, 0)),
            pl.BlockSpec((cut, hid), lambda i: (i, 0)),
            pl.BlockSpec((hid, cut), lambda i: (0, i)),
        ],
        out_shape=[
            jax.ShapeDtypeStruct((width, hid), BF16),
            jax.ShapeDtypeStruct((width, hid), BF16),
            jax.ShapeDtypeStruct((hid, width), BF16),
        ],
        scratch_shapes=[flat, rows, rows, row_tiles, row_tiles, column_tiles],
        compiler_params=params,
    )(tok, res, hidden, d_gate, d_up, mask)

    return (
        student.reshape(mine, width),
        token_grad.reshape(mine, width),
        grad_gate,
        grad_up,
        grad_down,
    )


def solution(mesh):
    placed = (
        P(("cand", "hid"), None),
        P(("cand", "hid"), None),
        P(None, "hid"),
        P(None, "hid"),
        P("hid", None),
        P(None, "hid", None),
        P("cand", "hid", None),
        P("cand"),
    )
    return jax.shard_map(
        functools.partial(per_device, mesh.shape["hid"]),
        mesh=mesh,
        in_specs=placed,
        out_specs=(
            P(("cand", "hid"), None),
            P(("cand", "hid"), None),
            P("cand", "hid"),
            P("cand", "hid"),
            P(("cand", "hid"), None),
        ),
        check_vma=False,
    )
```

```python
import functools

import jax
import jax.numpy as jnp
from jax import lax
from jax.experimental import pallas as pl
from jax.experimental.pallas import tpu as pltpu
from jax.sharding import PartitionSpec as P

BLOCK = 128
VMEM_BYTES = 60 * 1024 * 1024
F32 = jnp.float32
BF16 = jnp.bfloat16
AHEAD = 3


def peer(index):
    return (lax.axis_index("cand"), index)


def greet(chips):
    me = lax.axis_index("hid")
    chip, core = me // 2, me % 2
    barrier = pltpu.get_barrier_semaphore()
    for k in range(1, chips):
        pl.semaphore_signal(
            barrier,
            inc=1,
            device_id=peer(2 * lax.rem(chip + k, chips) + core),
            device_id_type=pl.DeviceIdType.MESH,
        )
    pl.semaphore_signal(
        barrier, inc=1, device_id=peer(2 * chip + 1 - core), device_id_type=pl.DeviceIdType.MESH
    )
    pl.semaphore_wait(barrier, chips)


def remote(src, dst, send_sem, recv_sem, index):
    return pltpu.make_async_remote_copy(
        src_ref=src,
        dst_ref=dst,
        send_sem=send_sem,
        recv_sem=recv_sem,
        device_id=peer(index),
        device_id_type=pl.DeviceIdType.MESH,
    )


def gather_blocks(chips, held, far_send, far_recv, near_send, near_recv):
    me = lax.axis_index("hid")
    chip, core = me // 2, me % 2
    beside = 2 * chip + 1 - core
    started = []
    for k in range(1, chips):
        to = 2 * lax.rem(chip + k, chips) + core
        copy = remote(held.at[me], held.at[me], far_send.at[k], far_recv.at[k], to)
        copy.start()
        started.append(copy)
    own = remote(held.at[me], held.at[me], near_send.at[0], near_recv.at[0], beside)
    own.start()
    passed = [own]
    for k in range(1, chips):
        source = 2 * lax.rem(chip - k + chips, chips) + core
        arrived = remote(
            held.at[source], held.at[source], far_send.at[k], far_recv.at[k], source
        )
        arrived.wait_recv()
        onward = remote(
            held.at[source], held.at[source], near_send.at[k], near_recv.at[k], beside
        )
        onward.start()
        passed.append(onward)
    for k in range(chips):
        block = 2 * lax.rem(chip - k + chips, chips) + 1 - core
        remote(
            held.at[block], held.at[block], near_send.at[k], near_recv.at[k], beside
        ).wait_recv()
    for copy in started + passed:
        copy.wait_send()


def scatter_sum(chips, part, near_in, out_slot, far_in, far_send, far_recv, near_send, near_recv):
    me = lax.axis_index("hid")
    chip, core = me // 2, me % 2
    beside = 2 * chip + 1 - core
    near = []
    for k in range(1, chips + 1):
        to = lax.rem(chip + k, chips)
        copy = remote(
            part.at[1 - core, to], near_in.at[to], near_send.at[k - 1], near_recv.at[k - 1], beside
        )
        copy.start()
        near.append(copy)
    far = []
    for k in range(1, chips):
        to = lax.rem(chip + k, chips)
        near[k - 1].wait_recv()
        out_slot[k] = (part[core, to].astype(F32) + near_in[to].astype(F32)).astype(BF16)
        copy = remote(
            out_slot.at[k], far_in.at[k], far_send.at[k], far_recv.at[k], 2 * to + core
        )
        copy.start()
        far.append(copy)
    near[chips - 1].wait_recv()
    total = part[core, chip].astype(F32) + near_in[chip].astype(F32)
    for k in range(1, chips):
        far[k - 1].wait_recv()
        total = total + far_in[k].astype(F32)
    for copy in near + far:
        copy.wait_send()
    return total


def gather_kernel(chips, own, out, held, line, fs, fr, ns, nr):
    unroll_tokens(own[...].astype(F32), line)
    held[lax.axis_index("hid")] = line[...].astype(BF16)
    greet(chips)
    gather_blocks(chips, held, fs, fr, ns, nr)
    out[...] = held[...]


def residual_kernel(
    chips, part, teacher, student, out, held, near_in, out_slot, far_in, line, fs, fr, ns, nr, fs2, fr2, ns2, nr2
):
    greet(chips)
    total = scatter_sum(chips, part, near_in, out_slot, far_in, fs, fr, ns, nr)
    unroll_tokens(teacher[...].astype(F32), line)
    held[lax.axis_index("hid")] = (total - line[...]).astype(BF16)
    line[...] = total
    roll_tokens(line, student)
    gather_blocks(chips, held, fs2, fr2, ns2, nr2)
    out[...] = held[...]


def scatter_kernel(chips, part, out, near_in, out_slot, far_in, line, fs, fr, ns, nr):
    greet(chips)
    line[...] = scatter_sum(chips, part, near_in, out_slot, far_in, fs, fr, ns, nr)
    roll_tokens(line, out)


def link_sems(chips):
    return [pltpu.SemaphoreType.DMA((chips,))] * 4


def in_vmem(count):
    return [pl.BlockSpec(memory_space=pltpu.VMEM)] * count


def exchange(body, operands, out_shape, scratch, cid):
    return pl.pallas_call(
        body,
        out_shape=out_shape,
        in_specs=in_vmem(len(operands)),
        out_specs=jax.tree.map(lambda _: pl.BlockSpec(memory_space=pltpu.VMEM), out_shape),
        scratch_shapes=scratch,
        compiler_params=pltpu.CompilerParams(collective_id=cid, has_side_effects=True),
    )(*operands)


def contract_first(left, right):
    return lax.dot_general(
        left, right, (((0,), (0,)), ((), ())), preferred_element_type=F32
    )


def contract_last(left, right):
    return lax.dot_general(
        left, right, (((1,), (1,)), ((), ())), preferred_element_type=F32
    )


def one_hot(tiles, width):
    row = lax.broadcasted_iota(jnp.int32, (tiles, width), 0)
    column = lax.broadcasted_iota(jnp.int32, (tiles, width), 1)
    return (column // BLOCK == row).astype(F32).astype(BF16)


def spread_rows(tiles, into):
    count, per, wide = into.shape
    full = contract_first(tiles, one_hot(tiles.shape[0], wide))
    for g in range(count):
        into[g] = full[g * per : (g + 1) * per]


def spread_columns(tiles, into):
    count, per, wide = into.shape
    for g in range(count):
        cut = wide // BLOCK
        into[g] = jnp.dot(
            tiles[:, g * cut : (g + 1) * cut],
            one_hot(cut, wide),
            preferred_element_type=F32,
        )


def clipped(weight, bounds):
    pieces = []
    for j in range(weight.shape[0] // BLOCK):
        bound = bounds[j : j + 1].astype(BF16)
        piece = weight[j * BLOCK : (j + 1) * BLOCK]
        pieces.append(jnp.maximum(jnp.minimum(piece, bound), -bound))
    return jnp.concatenate(pieces, axis=0) if len(pieces) > 1 else pieces[0]


def to_rows(blocks, flat, into):
    tokens, tiles = blocks.shape[0], blocks.shape[1]
    flat[...] = blocks[...].astype(F32).reshape(flat.shape)
    count, _, wide = into.shape
    cut = wide // BLOCK
    for w in range(tiles):
        piece = flat[pl.ds(w, tokens, stride=tiles), :].astype(BF16)
        into[w // cut, :, (w % cut) * BLOCK : (w % cut + 1) * BLOCK] = piece


def put_columns(flat, value, first, tiles):
    tokens = value.shape[0]
    for j in range(value.shape[1] // BLOCK):
        flat[pl.ds(first + j, tokens, stride=tiles), :] = value[:, j * BLOCK : (j + 1) * BLOCK]


def to_shares(flat, out):
    _, chips, per, _ = out.shape
    for d in range(2 * chips):
        out[d % 2, d // 2] = flat[d * per : (d + 1) * per].astype(BF16)


def bounds_of(scale, mask, width, bg, bu, bd):
    for m, into in enumerate((bg, bu, bd)):
        level = (jnp.left_shift(1, width[m] - 1) - 1).astype(F32)
        tiles = (scale[m] * level * mask[m].astype(F32)).astype(BF16)
        if m < 2:
            spread_rows(tiles, into)
        else:
            spread_columns(tiles, into)


def in_pairs(steps, cut, wg, wu, gate_w, up_w, sems, i):
    rows = pl.ds(pl.multiple_of(i * cut, cut), cut)
    return (
        pltpu.make_async_copy(wg.at[rows], gate_w.at[i], sems.at[0, i]),
        pltpu.make_async_copy(wu.at[rows], up_w.at[i], sems.at[1, i]),
    )


def in_down(steps, cut, wd, down_w, sems, i):
    columns = pl.ds(pl.multiple_of(i * cut, cut), cut)
    return pltpu.make_async_copy(wd.at[:, columns], down_w.at[i], sems.at[2, i])


def unroll_tokens(tokens, flat):
    count, width = tokens.shape
    tiles = width // BLOCK
    for t in range(count):
        for w in range(tiles):
            flat[t * tiles + w : t * tiles + w + 1, :] = tokens[
                t : t + 1, w * BLOCK : (w + 1) * BLOCK
            ]


def roll_tokens(flat, out):
    count, width = out.shape
    tiles = width // BLOCK
    for w in range(tiles):
        pieces = [flat[t * tiles + w : t * tiles + w + 1, :] for t in range(count)]
        piece = jnp.concatenate(pieces, axis=0) if count > 1 else pieces[0]
        out[:, w * BLOCK : (w + 1) * BLOCK] = piece.astype(BF16)


def start_all(copies):
    for copy in copies:
        copy.start()


def forward_products(
    steps, cut, tiles, rows, weights, held_w, sems, bg, bu, bd, gate_pre, up_pre, hidden, flat, keep
):
    wg, wu, wd = weights
    gate_w, up_w, down_w = held_w
    pair = functools.partial(in_pairs, steps, cut, wg, wu, gate_w, up_w, sems)
    down = functools.partial(in_down, steps, cut, wd, down_w, sems)
    ahead = min(AHEAD, steps)
    gate_pre[...] = jnp.zeros_like(gate_pre)
    up_pre[...] = jnp.zeros_like(up_pre)

    @pl.loop(0, steps)
    def _(i):
        @pl.when(i + ahead < steps)
        def _():
            start_all(pair(i + ahead))

        @pl.when(i + ahead >= steps)
        def _():
            start_all([down(2 * (i + ahead - steps)), down(2 * (i + ahead - steps) + 1)])

        for copy in pair(i):
            copy.wait()
        for source, bound, into in ((gate_w, bg, gate_pre), (up_w, bu, up_pre)):
            value = clipped(source[i], bound[i])
            if keep:
                source[i] = value
            into[...] += jnp.dot(rows[i], value, preferred_element_type=F32)

    gate = gate_pre[...]
    hidden[...] = (gate * jax.nn.sigmoid(gate) * up_pre[...]).astype(BF16)

    @pl.loop(0, steps)
    def _(c):
        @pl.when(c + 2 * ahead < steps)
        def _():
            down(c + 2 * ahead).start()

        down(c).wait()
        kept = clipped(down_w[c], bd[c])
        if keep:
            down_w[c] = kept
        value = jnp.dot(hidden[...], kept, preferred_element_type=F32)
        put_columns(flat, value, c * (cut // BLOCK), tiles)


def backward_products(
    steps, cut, tiles, rows, held_w, gate_pre, up_pre, d_hidden, d_gate, d_up, flat, ready_down, ready_pair
):
    gate_w, up_w, down_w = held_w
    d_hidden[...] = jnp.zeros_like(d_hidden)

    @pl.loop(0, steps)
    def _(c):
        d_hidden[...] += contract_last(rows[c], ready_down(c))

    gate = gate_pre[...]
    sig = jax.nn.sigmoid(gate)
    d_gate[...] = (d_hidden[...] * up_pre[...] * sig * (1.0 + gate * (1.0 - sig))).astype(BF16)
    d_up[...] = (d_hidden[...] * (gate * sig)).astype(BF16)

    @pl.loop(0, steps)
    def _(i):
        gate_i, up_i = ready_pair(i)
        value = contract_last(d_gate[...], gate_i) + contract_last(d_up[...], up_i)
        put_columns(flat, value, i * (cut // BLOCK), tiles)


def forward_kernel(
    steps, cut, tiles, width, tok, wg, wu, wd, scale, mask, part, gate_pre, up_pre, hidden,
    flat, rows, bg, bu, bd, gate_w, up_w, down_w, sems
):
    held_w = (gate_w, up_w, down_w)
    for i in range(min(AHEAD, steps)):
        start_all(in_pairs(steps, cut, wg, wu, gate_w, up_w, sems, i))
    to_rows(tok, flat, rows)
    bounds_of(scale, mask, width, bg, bu, bd)
    forward_products(
        steps, cut, tiles, rows, (wg, wu, wd), held_w, sems, bg, bu, bd,
        gate_pre, up_pre, hidden, flat, False,
    )
    to_shares(flat, part)


def backward_kernel(
    steps, cut, tiles, width, res, wg, wu, wd, scale, mask, gate_pre, up_pre, part, d_gate, d_up,
    flat, rows, bg, bu, bd, gate_w, up_w, down_w, sems, d_hidden
):
    pair = functools.partial(in_pairs, steps, cut, wg, wu, gate_w, up_w, sems)
    down = functools.partial(in_down, steps, cut, wd, down_w, sems)
    ahead = min(2 * AHEAD, steps)
    for c in range(ahead):
        down(c).start()
    to_rows(res, flat, rows)
    bounds_of(scale, mask, width, bg, bu, bd)

    def ready_down(c):
        @pl.when(c + ahead < steps)
        def _():
            down(c + ahead).start()

        @pl.when(c + ahead >= steps)
        def _():
            start_all(pair(c + ahead - steps))

        down(c).wait()
        return clipped(down_w[c], bd[c])

    def ready_pair(i):
        @pl.when(i + ahead < steps)
        def _():
            start_all(pair(i + ahead))

        for copy in pair(i):
            copy.wait()
        return clipped(gate_w[i], bg[i]), clipped(up_w[i], bu[i])

    backward_products(
        steps, cut, tiles, rows, (gate_w, up_w, down_w), gate_pre, up_pre, d_hidden, d_gate, d_up,
        flat, ready_down, ready_pair,
    )
    to_shares(flat, part)


def outer(left, right, mask, out):
    for j in range(left.shape[1] // BLOCK):
        kept = right * mask[j : j + 1].astype(BF16)
        out[j * BLOCK : (j + 1) * BLOCK] = contract_first(
            left[:, j * BLOCK : (j + 1) * BLOCK], kept
        ).astype(BF16)


def grad_kernel(tok, res, hidden, d_gate, d_up, mask, gg, gu, gd, flat, rows, rows2, mg, mu, md):
    i = pl.program_id(0)

    @pl.when(i == 0)
    def _():
        to_rows(tok, flat, rows)
        to_rows(res, flat, rows2)
        spread_rows(mask[0].astype(F32).astype(BF16), mg)
        spread_rows(mask[1].astype(F32).astype(BF16), mu)
        spread_columns(mask[2].astype(F32).astype(BF16), md)

    outer(rows[i], d_gate[...], mg[i], gg)
    outer(rows[i], d_up[...], mu[i], gu)
    outer(hidden[...], rows2[i], md[i], gd)


def per_device(n, tokens, teacher, w_gate, w_up, w_down, tile_scale, block_mask, bit_width):
    chips = n // 2
    mine, width = tokens.shape
    tiles = width // BLOCK
    all_tokens = n * mine
    hid = w_gate.shape[1]
    hid_tiles = hid // BLOCK
    cut = 1024
    steps = width // cut
    per = cut // BLOCK
    share = mine * tiles

    block = jax.ShapeDtypeStruct((mine, width), BF16)
    line = pltpu.VMEM((share, BLOCK), F32)
    blocks = jax.ShapeDtypeStruct((n, share, BLOCK), BF16)
    held = pltpu.VMEM((n, share, BLOCK), BF16)
    some = pltpu.VMEM((chips, share, BLOCK), BF16)

    tok = exchange(
        functools.partial(gather_kernel, chips),
        (tokens,),
        blocks,
        [held, line] + link_sems(chips),
        0,
    ).reshape(all_tokens, tiles, BLOCK)

    whole = lambda shape: pl.BlockSpec(shape, lambda i: (0,) * len(shape))
    tok_spec = whole((all_tokens, tiles, BLOCK))
    pre_spec = whole((all_tokens, hid))
    part_shape = (2, chips, share, BLOCK)
    bound_spec = whole((3, hid_tiles, tiles))
    flat = pltpu.VMEM((all_tokens * tiles, BLOCK), F32)
    rows = pltpu.VMEM((steps, all_tokens, cut), BF16)
    row_tiles = pltpu.VMEM((steps, per, hid), F32)
    column_tiles = pltpu.VMEM((steps, hid_tiles, cut), F32)
    params = pltpu.CompilerParams(
        dimension_semantics=("arbitrary",), vmem_limit_bytes=VMEM_BYTES
    )
    pre = jax.ShapeDtypeStruct((all_tokens, hid), F32)
    low = jax.ShapeDtypeStruct((all_tokens, hid), BF16)

    anywhere = pl.BlockSpec(memory_space=pl.ANY)
    vmem = pl.BlockSpec(memory_space=pltpu.VMEM)
    smem = pl.BlockSpec(memory_space=pltpu.SMEM)
    plain = pltpu.CompilerParams(vmem_limit_bytes=VMEM_BYTES)
    stores = [
        pltpu.VMEM((steps, cut, hid), BF16),
        pltpu.VMEM((steps, cut, hid), BF16),
        pltpu.VMEM((steps, hid, cut), BF16),
        pltpu.SemaphoreType.DMA((3, steps)),
    ]
    part, gate_pre, up_pre, hidden = pl.pallas_call(
        functools.partial(forward_kernel, steps, cut, tiles),
        in_specs=[smem, vmem, anywhere, anywhere, anywhere, vmem, vmem],
        out_specs=[vmem] * 4,
        out_shape=[jax.ShapeDtypeStruct(part_shape, BF16), pre, pre, low],
        scratch_shapes=[flat, rows, row_tiles, row_tiles, column_tiles] + stores,
        compiler_params=plain,
    )(bit_width, tok, w_gate, w_up, w_down, tile_scale, block_mask)

    student, res = exchange(
        functools.partial(residual_kernel, chips),
        (part, teacher),
        (block, blocks),
        [held, some, some, some, line] + link_sems(chips) + link_sems(chips),
        1,
    )
    res = res.reshape(all_tokens, tiles, BLOCK)

    part, d_gate, d_up = pl.pallas_call(
        functools.partial(backward_kernel, steps, cut, tiles),
        in_specs=[smem, vmem, anywhere, anywhere, anywhere, vmem, vmem, vmem, vmem],
        out_specs=[vmem] * 3,
        out_shape=[jax.ShapeDtypeStruct(part_shape, BF16), low, low],
        scratch_shapes=[flat, rows, row_tiles, row_tiles, column_tiles]
        + stores
        + [pltpu.VMEM((all_tokens, hid), F32)],
        compiler_params=plain,
    )(bit_width, res, w_gate, w_up, w_down, tile_scale, block_mask, gate_pre, up_pre)

    token_grad = exchange(
        functools.partial(scatter_kernel, chips),
        (part,),
        block,
        [some, some, some, line] + link_sems(chips),
        2,
    )

    grad_gate, grad_up, grad_down = pl.pallas_call(
        grad_kernel,
        grid=(steps,),
        in_specs=[tok_spec, tok_spec, pre_spec, pre_spec, pre_spec, bound_spec],
        out_specs=[
            pl.BlockSpec((cut, hid), lambda i: (i, 0)),
            pl.BlockSpec((cut, hid), lambda i: (i, 0)),
            pl.BlockSpec((hid, cut), lambda i: (0, i)),
        ],
        out_shape=[
            jax.ShapeDtypeStruct((width, hid), BF16),
            jax.ShapeDtypeStruct((width, hid), BF16),
            jax.ShapeDtypeStruct((hid, width), BF16),
        ],
        scratch_shapes=[flat, rows, rows, row_tiles, row_tiles, column_tiles],
        compiler_params=params,
    )(tok, res, hidden, d_gate, d_up, block_mask)

    return (
        student,
        token_grad,
        grad_gate,
        grad_up,
        grad_down,
    )


def solution(mesh):
    placed = (
        P(("cand", "hid"), None),
        P(("cand", "hid"), None),
        P(None, "hid"),
        P(None, "hid"),
        P("hid", None),
        P(None, "hid", None),
        P("cand", "hid", None),
        P("cand"),
    )
    return jax.shard_map(
        functools.partial(per_device, mesh.shape["hid"]),
        mesh=mesh,
        in_specs=placed,
        out_specs=(
            P(("cand", "hid"), None),
            P(("cand", "hid"), None),
            P("cand", "hid"),
            P("cand", "hid"),
            P(("cand", "hid"), None),
        ),
        check_vma=False,
    )
```

```python
import functools

import jax
import jax.numpy as jnp
from jax import lax
from jax.experimental import pallas as pl
from jax.experimental.pallas import tpu as pltpu
from jax.sharding import PartitionSpec as P

BLOCK = 128
VMEM_BYTES = 60 * 1024 * 1024
F32 = jnp.float32
BF16 = jnp.bfloat16
AHEAD = 3


def peer(index):
    return (lax.axis_index("cand"), index)


def greet(chips):
    me = lax.axis_index("hid")
    chip, core = me // 2, me % 2
    barrier = pltpu.get_barrier_semaphore()
    for k in range(1, chips):
        pl.semaphore_signal(
            barrier,
            inc=1,
            device_id=peer(2 * lax.rem(chip + k, chips) + core),
            device_id_type=pl.DeviceIdType.MESH,
        )
    pl.semaphore_signal(
        barrier, inc=1, device_id=peer(2 * chip + 1 - core), device_id_type=pl.DeviceIdType.MESH
    )
    pl.semaphore_wait(barrier, chips)


def remote(src, dst, send_sem, recv_sem, index):
    return pltpu.make_async_remote_copy(
        src_ref=src,
        dst_ref=dst,
        send_sem=send_sem,
        recv_sem=recv_sem,
        device_id=peer(index),
        device_id_type=pl.DeviceIdType.MESH,
    )


def gather_blocks(chips, held, far_send, far_recv, near_send, near_recv):
    me = lax.axis_index("hid")
    chip, core = me // 2, me % 2
    beside = 2 * chip + 1 - core
    started = []
    for k in range(1, chips):
        to = 2 * lax.rem(chip + k, chips) + core
        copy = remote(held.at[me], held.at[me], far_send.at[k], far_recv.at[k], to)
        copy.start()
        started.append(copy)
    own = remote(held.at[me], held.at[me], near_send.at[0], near_recv.at[0], beside)
    own.start()
    passed = [own]
    for k in range(1, chips):
        source = 2 * lax.rem(chip - k + chips, chips) + core
        arrived = remote(
            held.at[source], held.at[source], far_send.at[k], far_recv.at[k], source
        )
        arrived.wait_recv()
        onward = remote(
            held.at[source], held.at[source], near_send.at[k], near_recv.at[k], beside
        )
        onward.start()
        passed.append(onward)
    for k in range(chips):
        block = 2 * lax.rem(chip - k + chips, chips) + 1 - core
        remote(
            held.at[block], held.at[block], near_send.at[k], near_recv.at[k], beside
        ).wait_recv()
    for copy in started + passed:
        copy.wait_send()


def scatter_sum(chips, part, near_in, out_slot, far_in, far_send, far_recv, near_send, near_recv):
    me = lax.axis_index("hid")
    chip, core = me // 2, me % 2
    beside = 2 * chip + 1 - core
    near = []
    for k in range(1, chips + 1):
        to = lax.rem(chip + k, chips)
        copy = remote(
            part.at[1 - core, to], near_in.at[to], near_send.at[k - 1], near_recv.at[k - 1], beside
        )
        copy.start()
        near.append(copy)
    far = []
    for k in range(1, chips):
        to = lax.rem(chip + k, chips)
        near[k - 1].wait_recv()
        out_slot[k] = (part[core, to].astype(F32) + near_in[to].astype(F32)).astype(BF16)
        copy = remote(
            out_slot.at[k], far_in.at[k], far_send.at[k], far_recv.at[k], 2 * to + core
        )
        copy.start()
        far.append(copy)
    near[chips - 1].wait_recv()
    total = part[core, chip].astype(F32) + near_in[chip].astype(F32)
    for k in range(1, chips):
        far[k - 1].wait_recv()
        total = total + far_in[k].astype(F32)
    for copy in near + far:
        copy.wait_send()
    return total


def link_sems(chips):
    return [pltpu.SemaphoreType.DMA((chips,))] * 4


def contract_first(left, right):
    return lax.dot_general(
        left, right, (((0,), (0,)), ((), ())), preferred_element_type=F32
    )


def contract_last(left, right):
    return lax.dot_general(
        left, right, (((1,), (1,)), ((), ())), preferred_element_type=F32
    )


def one_hot(tiles, width):
    row = lax.broadcasted_iota(jnp.int32, (tiles, width), 0)
    column = lax.broadcasted_iota(jnp.int32, (tiles, width), 1)
    return (column // BLOCK == row).astype(F32).astype(BF16)


def spread_rows(tiles, into):
    count, per, wide = into.shape
    full = contract_first(tiles, one_hot(tiles.shape[0], wide))
    for g in range(count):
        into[g] = full[g * per : (g + 1) * per]


def spread_columns(tiles, into):
    count, per, wide = into.shape
    for g in range(count):
        cut = wide // BLOCK
        into[g] = jnp.dot(
            tiles[:, g * cut : (g + 1) * cut],
            one_hot(cut, wide),
            preferred_element_type=F32,
        )


def clipped(weight, bounds):
    pieces = []
    for j in range(weight.shape[0] // BLOCK):
        bound = bounds[j : j + 1].astype(BF16)
        piece = weight[j * BLOCK : (j + 1) * BLOCK]
        pieces.append(jnp.maximum(jnp.minimum(piece, bound), -bound))
    return jnp.concatenate(pieces, axis=0) if len(pieces) > 1 else pieces[0]


def to_rows(blocks, flat, into):
    flat[...] = blocks[...].astype(F32).reshape(flat.shape)
    count, tokens, wide = into.shape
    tiles = count * wide // BLOCK
    cut = wide // BLOCK
    for w in range(tiles):
        piece = flat[pl.ds(w, tokens, stride=tiles), :].astype(BF16)
        into[w // cut, :, (w % cut) * BLOCK : (w % cut + 1) * BLOCK] = piece


def put_columns(flat, value, first, tiles):
    tokens = value.shape[0]
    for j in range(value.shape[1] // BLOCK):
        flat[pl.ds(first + j, tokens, stride=tiles), :] = value[:, j * BLOCK : (j + 1) * BLOCK]


def to_shares(flat, out):
    _, chips, per, _ = out.shape
    for d in range(2 * chips):
        out[d % 2, d // 2] = flat[d * per : (d + 1) * per].astype(BF16)


def bounds_of(scale, mask, width, bg, bu, bd):
    for m, into in enumerate((bg, bu, bd)):
        level = (jnp.left_shift(1, width[m] - 1) - 1).astype(F32)
        tiles = (scale[m] * level * mask[m].astype(F32)).astype(BF16)
        if m < 2:
            spread_rows(tiles, into)
        else:
            spread_columns(tiles, into)


def in_pairs(steps, cut, wg, wu, gate_w, up_w, sems, i):
    rows = pl.ds(pl.multiple_of(i * cut, cut), cut)
    return (
        pltpu.make_async_copy(wg.at[rows], gate_w.at[i], sems.at[0, i]),
        pltpu.make_async_copy(wu.at[rows], up_w.at[i], sems.at[1, i]),
    )


def in_down(steps, cut, wd, down_w, sems, i):
    columns = pl.ds(pl.multiple_of(i * cut, cut), cut)
    return pltpu.make_async_copy(wd.at[:, columns], down_w.at[i], sems.at[2, i])


def unroll_tokens(tokens, flat):
    count, width = tokens.shape
    tiles = width // BLOCK
    for t in range(count):
        for w in range(tiles):
            flat[t * tiles + w : t * tiles + w + 1, :] = tokens[
                t : t + 1, w * BLOCK : (w + 1) * BLOCK
            ]


def roll_tokens(flat, out):
    count, width = out.shape
    tiles = width // BLOCK
    for w in range(tiles):
        pieces = [flat[t * tiles + w : t * tiles + w + 1, :] for t in range(count)]
        piece = jnp.concatenate(pieces, axis=0) if count > 1 else pieces[0]
        out[:, w * BLOCK : (w + 1) * BLOCK] = piece.astype(BF16)


def start_all(copies):
    for copy in copies:
        copy.start()


def forward_products(
    steps, cut, tiles, rows, weights, held_w, sems, bg, bu, bd, gate_pre, up_pre, hidden, flat, keep
):
    wg, wu, wd = weights
    gate_w, up_w, down_w = held_w
    pair = functools.partial(in_pairs, steps, cut, wg, wu, gate_w, up_w, sems)
    down = functools.partial(in_down, steps, cut, wd, down_w, sems)
    ahead = min(AHEAD, steps)
    gate_pre[...] = jnp.zeros_like(gate_pre)
    up_pre[...] = jnp.zeros_like(up_pre)

    @pl.loop(0, steps)
    def _(i):
        @pl.when(i + ahead < steps)
        def _():
            start_all(pair(i + ahead))

        @pl.when(i + ahead >= steps)
        def _():
            start_all([down(2 * (i + ahead - steps)), down(2 * (i + ahead - steps) + 1)])

        for copy in pair(i):
            copy.wait()
        for source, bound, into in ((gate_w, bg, gate_pre), (up_w, bu, up_pre)):
            value = clipped(source[i], bound[i])
            if keep:
                source[i] = value
            into[...] += jnp.dot(rows[i], value, preferred_element_type=F32)

    gate = gate_pre[...]
    hidden[...] = (gate * jax.nn.sigmoid(gate) * up_pre[...]).astype(BF16)

    @pl.loop(0, steps)
    def _(c):
        @pl.when(c + 2 * ahead < steps)
        def _():
            down(c + 2 * ahead).start()

        down(c).wait()
        kept = clipped(down_w[c], bd[c])
        if keep:
            down_w[c] = kept
        value = jnp.dot(hidden[...], kept, preferred_element_type=F32)
        put_columns(flat, value, c * (cut // BLOCK), tiles)


def backward_products(
    steps, cut, tiles, rows, held_w, gate_pre, up_pre, d_hidden, d_gate, d_up, flat, ready_down, ready_pair
):
    gate_w, up_w, down_w = held_w
    d_hidden[...] = jnp.zeros_like(d_hidden)

    @pl.loop(0, steps)
    def _(c):
        d_hidden[...] += contract_last(rows[c], ready_down(c))

    gate = gate_pre[...]
    sig = jax.nn.sigmoid(gate)
    d_gate[...] = (d_hidden[...] * up_pre[...] * sig * (1.0 + gate * (1.0 - sig))).astype(BF16)
    d_up[...] = (d_hidden[...] * (gate * sig)).astype(BF16)

    @pl.loop(0, steps)
    def _(i):
        gate_i, up_i = ready_pair(i)
        value = contract_last(d_gate[...], gate_i) + contract_last(d_up[...], up_i)
        put_columns(flat, value, i * (cut // BLOCK), tiles)


def layer_kernel(
    chips, steps, cut, tiles, width, tokens, teacher, wg, wu, wd, scale, mask,
    student, token_grad, rows, res_rows, hidden, d_gate, d_up,
    gate_w, up_w, down_w, sems, flat, bg, bu, bd, gate_pre, up_pre, d_hidden, line, part,
    tok_held, near_1, slot_1, far_1, res_held, near_2, slot_2, far_2, *links
):
    held_w = (gate_w, up_w, down_w)
    for i in range(min(AHEAD, steps)):
        start_all(in_pairs(steps, cut, wg, wu, gate_w, up_w, sems, i))
    unroll_tokens(tokens[...].astype(F32), line)
    tok_held[lax.axis_index("hid")] = line[...].astype(BF16)
    greet(chips)
    bounds_of(scale, mask, width, bg, bu, bd)
    gather_blocks(chips, tok_held, *links[0:4])
    to_rows(tok_held, flat, rows)
    forward_products(
        steps, cut, tiles, rows, (wg, wu, wd), held_w, sems, bg, bu, bd,
        gate_pre, up_pre, hidden, flat, True,
    )
    to_shares(flat, part)
    total = scatter_sum(chips, part, near_1, slot_1, far_1, *links[4:8])
    unroll_tokens(teacher[...].astype(F32), line)
    res_held[lax.axis_index("hid")] = (total - line[...]).astype(BF16)
    line[...] = total
    roll_tokens(line, student)
    gather_blocks(chips, res_held, *links[8:12])
    to_rows(res_held, flat, res_rows)
    backward_products(
        steps, cut, tiles, res_rows, held_w, gate_pre, up_pre, d_hidden, d_gate, d_up, flat,
        lambda c: down_w[c],
        lambda i: (gate_w[i], up_w[i]),
    )
    to_shares(flat, part)
    line[...] = scatter_sum(chips, part, near_2, slot_2, far_2, *links[12:16])
    roll_tokens(line, token_grad)


def outer(left, right, mask, out):
    for j in range(left.shape[1] // BLOCK):
        kept = right * mask[j : j + 1].astype(BF16)
        out[j * BLOCK : (j + 1) * BLOCK] = contract_first(
            left[:, j * BLOCK : (j + 1) * BLOCK], kept
        ).astype(BF16)


def grad_kernel(rows, res_rows, hidden, d_gate, d_up, mask, gg, gu, gd, mg, mu, md):
    i = pl.program_id(0)

    @pl.when(i == 0)
    def _():
        spread_rows(mask[0].astype(F32).astype(BF16), mg)
        spread_rows(mask[1].astype(F32).astype(BF16), mu)
        spread_columns(mask[2].astype(F32).astype(BF16), md)

    outer(rows[i], d_gate[...], mg[i], gg)
    outer(rows[i], d_up[...], mu[i], gu)
    outer(hidden[...], res_rows[i], md[i], gd)


def per_device(n, tokens, teacher, w_gate, w_up, w_down, tile_scale, block_mask, bit_width):
    chips = n // 2
    mine, width = tokens.shape
    tiles = width // BLOCK
    all_tokens = n * mine
    hid = w_gate.shape[1]
    hid_tiles = hid // BLOCK
    cut = 1024
    steps = width // cut
    per = cut // BLOCK
    share = mine * tiles

    block = jax.ShapeDtypeStruct((mine, width), BF16)
    line = pltpu.VMEM((share, BLOCK), F32)
    held = pltpu.VMEM((n, share, BLOCK), BF16)
    some = pltpu.VMEM((chips, share, BLOCK), BF16)
    flat = pltpu.VMEM((all_tokens * tiles, BLOCK), F32)
    row_tiles = pltpu.VMEM((steps, per, hid), F32)
    column_tiles = pltpu.VMEM((steps, hid_tiles, cut), F32)
    pre = pltpu.VMEM((all_tokens, hid), F32)
    low = jax.ShapeDtypeStruct((all_tokens, hid), BF16)
    rows = jax.ShapeDtypeStruct((steps, all_tokens, cut), BF16)
    anywhere = pl.BlockSpec(memory_space=pl.ANY)
    vmem = pl.BlockSpec(memory_space=pltpu.VMEM)
    smem = pl.BlockSpec(memory_space=pltpu.SMEM)

    student, token_grad, tok_rows, res_rows, hidden, d_gate, d_up = pl.pallas_call(
        functools.partial(layer_kernel, chips, steps, cut, tiles),
        in_specs=[smem, vmem, vmem, anywhere, anywhere, anywhere, vmem, vmem],
        out_specs=[vmem] * 7,
        out_shape=[block, block, rows, rows, low, low, low],
        scratch_shapes=[
            pltpu.VMEM((steps, cut, hid), BF16),
            pltpu.VMEM((steps, cut, hid), BF16),
            pltpu.VMEM((steps, hid, cut), BF16),
            pltpu.SemaphoreType.DMA((3, steps)),
            flat, row_tiles, row_tiles, column_tiles, pre, pre, pre, line,
            pltpu.VMEM((2, chips, share, BLOCK), BF16),
            held, some, some, some, held, some, some, some,
        ]
        + link_sems(chips) * 4,
        compiler_params=pltpu.CompilerParams(
            collective_id=0, has_side_effects=True, vmem_limit_bytes=VMEM_BYTES
        ),
    )(bit_width, tokens, teacher, w_gate, w_up, w_down, tile_scale, block_mask)

    whole = lambda shape: pl.BlockSpec(shape, lambda i: (0,) * len(shape))
    pre_spec = whole((all_tokens, hid))
    row_spec = whole((steps, all_tokens, cut))
    grad_gate, grad_up, grad_down = pl.pallas_call(
        grad_kernel,
        grid=(steps,),
        in_specs=[row_spec, row_spec, pre_spec, pre_spec, pre_spec, whole(block_mask.shape)],
        out_specs=[
            pl.BlockSpec((cut, hid), lambda i: (i, 0)),
            pl.BlockSpec((cut, hid), lambda i: (i, 0)),
            pl.BlockSpec((hid, cut), lambda i: (0, i)),
        ],
        out_shape=[
            jax.ShapeDtypeStruct((width, hid), BF16),
            jax.ShapeDtypeStruct((width, hid), BF16),
            jax.ShapeDtypeStruct((hid, width), BF16),
        ],
        scratch_shapes=[row_tiles, row_tiles, column_tiles],
        compiler_params=pltpu.CompilerParams(
            dimension_semantics=("arbitrary",), vmem_limit_bytes=VMEM_BYTES
        ),
    )(tok_rows, res_rows, hidden, d_gate, d_up, block_mask)

    return (
        student,
        token_grad,
        grad_gate,
        grad_up,
        grad_down,
    )


def solution(mesh):
    placed = (
        P(("cand", "hid"), None),
        P(("cand", "hid"), None),
        P(None, "hid"),
        P(None, "hid"),
        P("hid", None),
        P(None, "hid", None),
        P("cand", "hid", None),
        P("cand"),
    )
    return jax.shard_map(
        functools.partial(per_device, mesh.shape["hid"]),
        mesh=mesh,
        in_specs=placed,
        out_specs=(
            P(("cand", "hid"), None),
            P(("cand", "hid"), None),
            P("cand", "hid"),
            P("cand", "hid"),
            P(("cand", "hid"), None),
        ),
        check_vma=False,
    )
```
